128 devices in a mesh: sec: 4 (over y_lo, core), tile: 32 (over y_hi, x, z).
Axes of the slice: x: 4, y: 4 (y_hi: 2, y_lo: 2; y = y_hi * 2 + y_lo), z: 4, core: 2. Of those that a mesh axis runs over, the one named last changes fastest.
Arguments:
- adjoint: float32 [4, 64, 256, 1024], P(None, None, 'tile', 'sec'), may hold values from -6 to 6
- kappa: float32 [63, 256, 1024], P(None, 'tile', 'sec'), may hold values from 0.1 to 600
- diffusion: float32 [256, 1024], P('tile', 'sec'), may hold values from 0.02 to 0.2
- gain: float32 [4], replicated, may hold values from 0.3 to 0.8
- store: bfloat16 [4, 1024, 4, 64, 256], P('sec', 'tile'), may hold values from -2.5 to 2.5
- sources: int32 [4, 256], P('sec'), may hold values from 0 to 1023, as said below
- ocean_mask: int32 [256, 256], P('tile'), may hold values 0 or 1
- remap: int32 [256, 256], P('tile'), may hold values from 0 to 6143, as said below
Outputs:
- result: float32 [4, 64, 256, 1024], P(None, None, 'tile', 'sec')
The draws below stay inside these ranges and needn't reach their ends.
Inputs may be any that keep to these rules, and one draw needn't show every extreme that they name: sources[s, d * 8 + j] // 32 is the tile index, in sec row s, of the device that holds reader (s, d)'s trajectory block j, and sources % 32 its slot there. Each holder that a reader uses gives it exactly 2 of its 8 blocks. remap[R, i] = k * 8 * 256 + r * 256 + c: the atmosphere cell at row r of the same tile's rows and column c of atmosphere section k + 1.
All inputs are finite; a program needn't handle non-finite values. No bound on the sum of `ocean_mask` on one device may be relied on, other than what follows from the above.
Results may differ from the reference program's by a relative error of at most 0.0006.
Values may be sent and summed in bfloat16 or wider, within the bound.
A program may use at most 128 MiB of HBM per device.

```python
import math
import jax
import jax.numpy as jnp
from jax import lax

F = 4
LEV = 64
ROWS = 8
LON = 256
BW = 256
SLOTS = 32
NB = 8
CAP = 2
NLAT = 256
NLON = 1024
N_SEC = 4
N_TILE = 32


def draw_sources(key, part):
    key = jax.random.fold_in(key, 11)
    key_hot, key_score, key_order, key_slot = jax.random.split(key, 4)
    groups = NB // CAP
    hot_holder = (jax.random.randint(key_hot, (N_SEC, N_TILE), 0, 6) == 0).astype(jnp.int32)
    score = jax.random.randint(key_score, (N_SEC, N_TILE, N_TILE), 0, 4096) + 3000 * hot_holder[:, None, :]
    score = score * N_TILE + jnp.arange(N_TILE, dtype=jnp.int32)
    _, chosen = lax.top_k(score, groups)
    holder = jnp.repeat(chosen.astype(jnp.int32), CAP, axis=-1)
    order_keys = jax.random.randint(key_order, (N_SEC, N_TILE, NB), 0, 1 << 20) * NB + jnp.arange(NB, dtype=jnp.int32)
    order = jnp.argsort(order_keys, axis=-1)
    holder = jnp.take_along_axis(holder, order, -1)
    slot = jax.random.randint(key_slot, (N_SEC, N_TILE, NB), 0, SLOTS)
    return (holder * SLOTS + slot).reshape(N_SEC, N_TILE * NB).astype(jnp.int32)


def draw_remap(key, part):
    key = jax.random.fold_in(key, 23)
    key_row, key_col = jax.random.split(key, 2)
    row_in = (jnp.arange(NLAT, dtype=jnp.int32) % ROWS)[:, None]
    col_in = jnp.arange(LON, dtype=jnp.int32)[None, :]
    jitter = jax.random.randint(key_row, (NLAT, LON), -1, 2)
    target_row = jnp.clip(row_in + jitter, 0, ROWS - 1)
    atmos_col = 3 * col_in + jax.random.randint(key_col, (NLAT, LON), 0, 3)
    section_part = atmos_col // LON
    return (section_part * ROWS * LON + target_row * LON + atmos_col % LON).astype(jnp.int32)


def draw_kappa(key, part):
    key = jax.random.fold_in(key, 37)
    key_column, key_level = jax.random.split(key, 2)
    column_low, column_high = (0.2, 150.0)
    column_level = jnp.exp(jax.random.uniform(key_column, (NLAT, NLON), jnp.float32, jnp.log(column_low), jnp.log(column_high)))
    roughness = jnp.exp(jax.random.uniform(key_level, (LEV - 1, NLAT, NLON), jnp.float32, jnp.log(0.5), jnp.log(2.0)))
    return (column_level[None] * roughness).astype(jnp.float32)


def plant(array, key, least, high):
    longest = array.shape.index(max(array.shape))
    spots = []
    for shift in (0, 1):
        where = [jax.random.randint(jax.random.fold_in(key, axis), (), 0, length) for axis, length in enumerate(array.shape)]
        where[longest] = (where[longest] + shift) % array.shape[longest]
        spots.append(tuple(where))
    return array.at[spots[0]].set(least).at[spots[1]].set(high)


def block_scale(key, extent, shards, low, top_value):
    def one(axis_at, blocks):
        draws = jax.random.uniform(jax.random.fold_in(jax.random.fold_in(key, 6), axis_at), (blocks,), jnp.float32, low / len(shards), top_value / len(shards))
        return jnp.repeat(jnp.exp(draws), extent[axis_at] // blocks).reshape((-1,) + (1,) * (len(extent) - axis_at - 1))

    loudness = one(*shards[0])
    for cut in shards[1:]:
        loudness = loudness * one(*cut)
    return loudness


def centred(key, extent, deviation, bound, cuts=(), kind=jnp.bfloat16):
    loudness = block_scale(key, extent, cuts, -0.22, 0.18) if cuts else 1.0
    values = jax.random.normal(key, extent, jnp.float32) * deviation * loudness
    return jnp.minimum(jnp.maximum(values, -bound), bound).astype(kind)


def setup_inputs(seed: int = 0) -> dict:
    key_list = jax.random.split(jax.random.key(seed), 9)
    adjoint = centred(key_list[0], (F, LEV, NLAT, NLON), 1.0, 6.0, ((2, 32), (3, 4)), jnp.float32)
    kappa = draw_kappa(jax.random.fold_in(key_list[8], 71), 0)
    diffusion = jnp.clip(jnp.exp(math.log(0.2) - 2.3025851 * jax.random.uniform(key_list[2], (NLAT, NLON), jnp.float32) ** block_scale(key_list[2], (NLAT, NLON), ((0, 32), (1, 4)), -0.2, 0.2)), 0.02, 0.2)
    gain = jnp.clip(jax.random.uniform(key_list[3], (F,), jnp.float32, 0.3, 0.8), 0.3, 0.8)
    store = centred(key_list[4], (N_SEC, N_TILE * SLOTS, 4, LEV, BW), 0.4, 2.5, ((0, 4), (1, 32)))
    sources = draw_sources(jax.random.fold_in(key_list[8], 71), 0)
    ocean_mask = plant((jax.random.randint(key_list[6], (NLAT, LON), 0, 10) < 7).astype(jnp.int32), jax.random.fold_in(key_list[6], 1), 0, 1)
    remap = draw_remap(jax.random.fold_in(key_list[8], 71), 0)
    return {"adjoint": adjoint, "kappa": kappa, "diffusion": diffusion, "gain": gain, "store": store, "sources": sources, "ocean_mask": ocean_mask, "remap": remap}


def column_solve(right, kappa):
    zero_layer = jnp.zeros_like(kappa[:1])
    below = jnp.concatenate([zero_layer, kappa], 0)
    above = jnp.concatenate([kappa, zero_layer], 0)
    main_coef = 1.0 + below + above
    moved = jnp.moveaxis(right, 1, 0)

    def forward(carry, inputs):
        prev_c, prev_d = carry
        lower_coef, middle, upper_coef, level_rhs = inputs
        denominator = middle + lower_coef * prev_c
        next_c = -upper_coef / denominator
        next_d = (level_rhs + lower_coef * prev_d) / denominator
        return (next_c, next_d), (next_c, next_d)

    start = (jnp.zeros_like(kappa[0]), jnp.zeros_like(moved[0]))
    _, (c_all, d_all) = lax.scan(forward, start, (below, main_coef, above, moved))

    def backward(later, inputs):
        c_level, d_level = inputs
        value = d_level - c_level * later
        return value, value

    _, solved = lax.scan(backward, jnp.zeros_like(moved[0]), (c_all, d_all), reverse=True)
    return jnp.moveaxis(solved, 0, 1)


def stencil(state, state_e, state_w, state_n, state_s, flux_e, flux_w, merid_n, merid_s, diffusion):
    return (state + diffusion * (state_e + state_w + state_n + state_s - 4.0 * state)
            + 0.5 * (flux_e - flux_w) + 0.5 * (merid_n - merid_s))


def shift_cycle(values, amount):
    ocean_part = jnp.roll(values[..., :LON], amount, -1)
    atmos_part = jnp.roll(values[..., LON:], amount, -1)
    return jnp.concatenate([ocean_part, atmos_part], -1)


def reference(adjoint, kappa, diffusion, gain, store, sources, ocean_mask, remap):
    pieces = []
    for section in range(N_SEC):
        blocks = store[section][sources[section]]
        blocks = blocks.reshape(N_TILE, NB, 4, LEV, BW).transpose(2, 3, 0, 1, 4)
        pieces.append(blocks.reshape(4, LEV, NLAT, LON))
    velocity = jnp.concatenate(pieces, 3)
    cell_count = ROWS * LON
    band_index = (jnp.arange(NLAT, dtype=jnp.int32) // ROWS)[:, None]
    sect_part = remap // cell_count
    local_part = remap % cell_count
    target_row = band_index * ROWS + local_part // LON
    target_col = sect_part * LON + local_part % LON
    sea = ocean_mask.astype(jnp.float32)
    sea_full = jnp.concatenate([sea, jnp.ones((NLAT, 3 * LON), jnp.float32)], 1)
    state = adjoint
    for step in range(2):
        ocean_top = state[:, 0, :, :LON]
        atmos_low = state[:, 0, :, LON:]
        ocean_add = gain[:, None, None] * sea * atmos_low[:, target_row, target_col]
        contrib = gain[:, None, None] * sea * ocean_top
        atmos_add = jnp.zeros_like(atmos_low).at[:, target_row, target_col].add(contrib)
        surface = jnp.concatenate([ocean_top + ocean_add, atmos_low + atmos_add], -1)
        state = state.at[:, 0].set(surface)
        mixed = column_solve(state, kappa)
        zonal = velocity[2 * step].astype(jnp.float32)
        meridional = velocity[2 * step + 1].astype(jnp.float32)
        zonal_flux = zonal * mixed
        merid_flux = meridional * mixed
        zero_row = jnp.zeros_like(mixed[:, :, :1])
        state_n = jnp.concatenate([mixed[:, :, 1:], zero_row], 2)
        state_s = jnp.concatenate([zero_row, mixed[:, :, :-1]], 2)
        merid_n = jnp.concatenate([merid_flux[:, :, 1:], zero_row], 2)
        merid_s = jnp.concatenate([zero_row, merid_flux[:, :, :-1]], 2)
        updated = stencil(mixed, shift_cycle(mixed, -1), shift_cycle(mixed, 1), state_n, state_s,
                          shift_cycle(zonal_flux, -1), shift_cycle(zonal_flux, 1), merid_n, merid_s, diffusion)
        state = updated * sea_full
    return state
```

```python
import functools

import jax
import jax.numpy as jnp
from jax import lax
from jax.experimental import pallas as pl
from jax.experimental.pallas import tpu as pltpu
from jax.sharding import PartitionSpec as P

F = 4
LEV = 64
ROWS = 8
LON = 256
NB = 8
SLOTS = 32
PLANE = LEV * ROWS
SIZE = {"y": 2, "x": 4, "z": 4}
ORDERS = (("x", "z", "y"), ("z", "y", "x"), ("y", "x", "z"))
PART_ROWS = (32, 48, 48)
PART_AT = (0, 32, 80)
MESH = pl.DeviceIdType.MESH
BF = jnp.bfloat16
F32 = jnp.float32
NT = (((1,), (1,)), ((), ()))
TN = (((0,), (0,)), ((), ()))


def coords(tile):
    return {"y": tile // 16, "x": (tile // 4) % 4, "z": tile % 4}


def tile_of(at):
    return at["y"] * 16 + at["x"] * 4 + at["z"]


def moved(at, axis, by):
    other = dict(at)
    other[axis] = lax.rem(at[axis] + by, SIZE[axis])
    return other


def rows_of(level):
    return pl.ds(pl.multiple_of(level * ROWS, ROWS), ROWS)


def wide(ref, at):
    return jnp.concatenate([ref[0, at, :], ref[1, at, :]], 1)


def put(ref, at, value):
    ref[0, at, :] = value[:, :128]
    ref[1, at, :] = value[:, 128:]


def kernel(adj, kappa, diff, store, mask, remap, gain, sources, out, *scratch):
    (store_v, st, mx, kap, inv, low, up, vel, diff_v, mask_v, remap_v, coef, dedge, cpl,
     s1, r1, r2, s3, r3, surf_s, surf_r, ew_s, ew_r, zw_s, zw_r, mr_s, mr_r, vr_s, vr_r,
     load_sem, out_sem, own_sem, e_send, e_recv, h_send, h_recv) = scratch
    tile = lax.axis_index("tile")
    sec = lax.axis_index("sec")
    me = coords(tile)

    loads = [
        pltpu.make_async_copy(adj.at[:, pl.ds(0, 128)], st.at[0], load_sem.at[0]),
        pltpu.make_async_copy(adj.at[:, pl.ds(128, 128)], st.at[1], load_sem.at[6]),
        pltpu.make_async_copy(store, store_v, load_sem.at[1]),
        pltpu.make_async_copy(kappa, kap.at[pl.ds(0, PLANE - ROWS)], load_sem.at[2]),
        pltpu.make_async_copy(diff, diff_v, load_sem.at[3]),
        pltpu.make_async_copy(mask, mask_v, load_sem.at[4]),
        pltpu.make_async_copy(remap, remap_v, load_sem.at[5]),
    ]
    for load in loads:
        load.start()

    barrier = pltpu.get_barrier_semaphore()
    greeted = 0
    for axis in ("x", "z", "y"):
        for by in range(1, SIZE[axis]):
            pl.semaphore_signal(barrier, inc=1, device_id={"tile": tile_of(moved(me, axis, by))},
                                device_id_type=MESH)
            greeted += 1
    for by in (1, 31):
        pl.semaphore_signal(barrier, inc=1, device_id={"tile": lax.rem(tile + by, 32)},
                            device_id_type=MESH)
        greeted += 1
    for by in (1, 2, 3):
        pl.semaphore_signal(barrier, inc=1, device_id={"sec": lax.rem(sec + by, 4)},
                            device_id_type=MESH)
        greeted += 1
    pl.semaphore_wait(barrier, greeted)

    pending = []
    arrivals = {}

    def send(key, src, dst, send_sem, recv_sem, device):
        copy = pltpu.make_async_remote_copy(src, dst, send_sem, recv_sem, device_id=device,
                                            device_id_type=MESH)
        copy.start()
        pending.append(copy)
        arrivals.setdefault(key, []).append(copy)

    def arrived(key):
        for copy in arrivals.pop(key):
            copy.wait_recv()

    hsem = [0]

    def small(key, src, dst, device):
        n = hsem[0]
        hsem[0] += 1
        send(key, src, dst, h_send.at[n], h_recv.at[n], device)

    def to_sections(key, src, dst):
        for by in (1, 2, 3):
            small(key, src, dst.at[sec], {"sec": lax.rem(sec + by, 4)})

    def to_north_south(key, src, dst):
        small(key, src.at[0], dst.at[0], {"tile": lax.rem(tile + 31, 32)})
        small(key, src.at[1], dst.at[1], {"tile": lax.rem(tile + 1, 32)})

    def esem(half, part, stage, by):
        return ((half * 3 + part) * 3 + stage) * 3 + by - 1

    def stage_one(half, part):
        a1, a2, a3 = ORDERS[part]
        n1, n2, n3 = SIZE[a1], SIZE[a2], SIZE[a3]
        rows = PART_ROWS[part]
        at = half * 128 + PART_AT[part]
        sbuf, rbuf = s1[half * 3 + part], r1[half * 3 + part]
        for by in list(range(1, n1)) + [0]:
            c1 = lax.rem(me[a1] + by, n1)

            def one_reader(i, _):
                c2, c3 = i // n3, lax.rem(i, n3)
                reader = tile_of({a1: c1, a2: c2, a3: c3})
                first = jnp.int32(0)
                second = jnp.int32(0)
                for j in range(NB):
                    source = sources[0, reader * NB + j]
                    mine = source // SLOTS == tile
                    second = jnp.where(mine, source % SLOTS, second)
                for j in reversed(range(NB)):
                    source = sources[0, reader * NB + j]
                    mine = source // SLOTS == tile
                    first = jnp.where(mine, source % SLOTS, first)
                for k, slot in ((0, first), (1, second)):
                    block = store_v[slot, at:at + rows, :]
                    if by:
                        sbuf[by - 1, c2, c3, k] = block
                    else:
                        rbuf[c2, me[a1], c3, k] = block
                return 0

            lax.fori_loop(0, n2 * n3, one_reader, 0)
            if by:
                n = esem(half, part, 0, by)
                send((half, part, 0), sbuf.at[by - 1], rbuf.at[:, me[a1]], e_send.at[n], e_recv.at[n],
                     {"tile": tile_of(moved(me, a1, by))})

    def stage_two(half, part):
        a1, a2, a3 = ORDERS[part]
        src, dst = r1[half * 3 + part], r2[half * 3 + part]
        arrived((half, part, 0))
        for by in range(1, SIZE[a2]):
            c2 = lax.rem(me[a2] + by, SIZE[a2])
            n = esem(half, part, 1, by)
            send((half, part, 1), src.at[c2], dst.at[me[a2]], e_send.at[n], e_recv.at[n],
                 {"tile": tile_of(moved(me, a2, by))})
        own = pltpu.make_async_copy(src.at[me[a2]], dst.at[me[a2]], own_sem.at[half * 3 + part])
        own.start()
        arrivals[("own", half, part)] = [own]

    def stage_three(half, part):
        a1, a2, a3 = ORDERS[part]
        n3 = SIZE[a3]
        src, sbuf, rbuf = r2[half * 3 + part], s3[half * 3 + part], r3[half * 3 + part]
        arrivals.pop(("own", half, part))[0].wait()
        arrived((half, part, 1))
        for by in list(range(1, n3)) + [0]:
            target = moved(me, a3, by)
            reader = tile_of(target)
            holders = [sources[0, reader * NB + j] // SLOTS for j in range(NB)]
            for j in range(NB):
                rank = jnp.int32(0)
                for i in range(j):
                    rank = rank + jnp.where(holders[i] == holders[j], 1, 0)
                holder = coords(holders[j])
                block = src[holder[a2], holder[a1], target[a3], jnp.minimum(rank, 1)]
                if by:
                    sbuf[by - 1, j] = block
                else:
                    rbuf[me[a3], j] = block
            if by:
                n = esem(half, part, 2, by)
                send((half, part, 2), sbuf.at[by - 1], rbuf.at[me[a3]], e_send.at[n], e_recv.at[n],
                     {"tile": reader})

    def assemble(half, part):
        a3 = ORDERS[part][2]
        arrived((half, part, 2))
        rows = PART_ROWS[part]
        for j in range(NB):
            holder = coords(sources[0, tile * NB + j] // SLOTS)
            block = r3[half * 3 + part][holder[a3], j]
            put(vel, pl.ds(PART_AT[part] * ROWS + j, rows, stride=ROWS), block.astype(F32))
            for side, edge in ((0, 0), (1, NB - 1)):
                if j == edge and part:
                    lo = max(PART_AT[part], LEV)
                    hi = PART_AT[part] + rows
                    vr_s[half][side, lo - LEV:hi - LEV, :] = block[lo - PART_AT[part]:]

    lane = lax.broadcasted_iota(jnp.int32, (ROWS, LON), 1)
    row = lax.broadcasted_iota(jnp.int32, (ROWS, LON), 0)

    def edge_pick(low_lane, high_lane, field=None):
        wanted = jnp.where(row % 2 == 0, low_lane, high_lane)
        pick = lane == wanted
        if field is not None:
            pick = pick & (row // 2 == field)
        return jnp.where(pick, 1.0, 0.0)

    def send_surface(step):
        for f in range(F):
            surf_s[step][pl.ds(f * ROWS, ROWS), :] = wide(st, pl.ds(f * PLANE, ROWS))
        to_sections(("surf", step), surf_s[step], surf_r[step])

    def prepare():
        kap[pl.ds(PLANE - ROWS, ROWS), :] = jnp.zeros((ROWS, LON), F32)

        def level(l, carry):
            g, below = carry
            at = rows_of(l)
            above = kap[at, :]
            p = 1.0 + below * g
            w = 1.0 / (p + above)
            inv[at, :] = w
            low[at, :] = below * w
            up[at, :] = above * w
            return p * w, above

        zero = jnp.zeros((ROWS, LON), F32)
        lax.fori_loop(0, LEV, level, (zero, zero))
        d = diff_v[...]
        is_ocean = sec == 0
        sea = jnp.where(is_ocean, mask_v[...].astype(F32), 1.0)
        east_ok = jnp.where(is_ocean | (lane != 0), 1.0, 0.0)
        west_ok = jnp.where(is_ocean | (lane != LON - 1), 1.0, 0.0)
        north_ok = jnp.where(row != 0, 1.0, 0.0)
        south_ok = jnp.where(row != ROWS - 1, 1.0, 0.0)
        coef[0] = pltpu.roll(d, 1, 1) * east_ok
        coef[1] = 0.5 * east_ok
        coef[2] = pltpu.roll(d, LON - 1, 1) * west_ok
        coef[3] = 0.5 * west_ok
        coef[4] = pltpu.roll(d, 1, 0) * north_ok
        coef[5] = 0.5 * north_ok
        coef[6] = pltpu.roll(d, ROWS - 1, 0) * south_ok
        coef[7] = 0.5 * south_ok
        coef[8] = 1.0 - 4.0 * d
        coef[9] = sea
        tiled = jnp.broadcast_to(d[None], (LEV, ROWS, LON)).reshape(PLANE, LON)
        dedge[...] = lax.dot_general(edge_pick(LON - 1, 0), tiled, NT,
                                     precision=lax.Precision.HIGHEST, preferred_element_type=F32)

    def couple(step):
        surf_r[step][sec] = surf_s[step][...]
        arrived(("surf", step))
        iota = lax.broadcasted_iota(jnp.int32, (128, LON), 0)

        def parts_of(r):
            cell = remap_v[r:r + 1, :]
            onehot = jnp.where(iota == (cell & 127), 1.0, 0.0).astype(BF)
            high = ((cell >> 11) << 4) + (((cell >> 7) & 1) << 3) + ((cell >> 8) & 7)
            return onehot, high, mask_v[r:r + 1, :].astype(F32)

        @pl.when(sec == 0)
        def _():
            table = jnp.concatenate(
                [surf_r[step][s + 1, f * ROWS:(f + 1) * ROWS, h * 128:(h + 1) * 128]
                 for f in range(F) for s in range(3) for h in range(2)], 0).astype(BF)
            iota48 = lax.broadcasted_iota(jnp.int32, (48, LON), 0)
            for r in range(ROWS):
                onehot, high, sea = parts_of(r)
                found = jnp.dot(table, onehot, preferred_element_type=F32)
                hit = iota48 == high
                for f in range(F):
                    value = jnp.sum(jnp.where(hit, found[f * 48:(f + 1) * 48], 0.0), 0, keepdims=True)
                    cpl[f * ROWS + r:f * ROWS + r + 1, :] = gain[f] * sea * value

        @pl.when(sec != 0)
        def _():
            iota16 = lax.broadcasted_iota(jnp.int32, (16, LON), 0)
            total = jnp.zeros((F * 16, 128), F32)
            for r in range(ROWS):
                onehot, high, sea = parts_of(r)
                hit = iota16 == high - (sec - 1) * 16
                spread = []
                for f in range(F):
                    value = gain[f] * sea * surf_r[step][0, f * ROWS + r:f * ROWS + r + 1, :]
                    spread.append(jnp.where(hit, value, 0.0))
                spread = jnp.concatenate(spread, 0).astype(BF)
                total = total + lax.dot_general(spread, onehot, NT, preferred_element_type=F32)
            for f in range(F):
                for h in range(2):
                    at = (f * 2 + h) * ROWS
                    cpl[f * ROWS:(f + 1) * ROWS, h * 128:(h + 1) * 128] = total[at:at + ROWS]

        for f in range(F):
            at = pl.ds(f * PLANE, ROWS)
            put(st, at, wide(st, at) + cpl[pl.ds(f * ROWS, ROWS), :])

    def solve():
        def forward(l, carry):
            at = rows_of(l)
            w, a = inv[at, :], low[at, :]
            result = []
            for f in range(F):
                here = rows_of(f * LEV + l)
                d = wide(st, here) * w + a * carry[f]
                put(mx, here, d)
                result.append(d)
            return tuple(result)

        def backward(i, carry):
            l = LEV - 1 - i
            e = up[rows_of(l), :]
            result = []
            for f in range(F):
                here = rows_of(f * LEV + l)
                x = wide(mx, here) + e * carry[f]
                put(mx, here, x)
                result.append(x)
            return tuple(result)

        zero = tuple(jnp.zeros((ROWS, LON), F32) for _ in range(F))
        lax.fori_loop(0, LEV, forward, zero)
        lax.fori_loop(0, LEV, backward, zero)

    def send_mixed(step):
        for side, edge in ((0, 0), (1, ROWS - 1)):
            for f in range(F):
                mr_s[step][side, f * LEV:(f + 1) * LEV, :] = wide(
                    mx, pl.ds(f * PLANE + edge, LEV, stride=ROWS)).astype(BF)
        to_north_south(("mr", step), mr_s[step], mr_r[step])
        total = jnp.zeros((ROWS, PLANE), F32)
        for f in range(F):
            total = total + lax.dot_general(
                edge_pick(0, LON - 1, f).astype(BF), wide(mx, pl.ds(f * PLANE, PLANE)).astype(BF), NT,
                preferred_element_type=F32)
        ew_s[step][...] = total
        to_sections(("ew", step), ew_s[step], ew_r[step])

    def send_velocity(step):
        to_north_south(("vr", step), vr_s[step], vr_r[step])
        zw_s[step][...] = lax.dot_general(edge_pick(0, LON - 1).astype(BF), wide(vel, pl.ds(0, PLANE)).astype(BF), NT,
                                          preferred_element_type=F32)
        to_sections(("zw", step), zw_s[step], zw_r[step])

    def stencil():
        def level(l, _):
            z = wide(vel, rows_of(l))
            v = wide(vel, rows_of(LEV + l))
            c_e = coef[0] + coef[1] * z
            c_w = coef[2] - coef[3] * z
            c_n = coef[4] + coef[5] * v
            c_s = coef[6] - coef[7] * v
            for f in range(F):
                here = rows_of(f * LEV + l)
                m = wide(mx, here)
                total = m * coef[8]
                total = total + pltpu.roll(m * c_e, LON - 1, 1)
                total = total + pltpu.roll(m * c_w, 1, 1)
                total = total + pltpu.roll(m * c_n, ROWS - 1, 0)
                total = total + pltpu.roll(m * c_s, 1, 0)
                put(st, here, total * coef[9])
            return 0

        lax.fori_loop(0, LEV, level, 0)

    def add_halos(step, done=None):
        arrived(("mr", step))
        arrived(("vr", step))
        arrived(("ew", step))
        arrived(("zw", step))
        even = lax.broadcasted_iota(jnp.int32, (ROWS, PLANE), 0) % 2 == 0
        east = jnp.where(sec >= 3, 1, sec + 1)
        west = jnp.where(sec <= 1, 3, sec - 1)
        m = jnp.where(even, ew_r[step][jnp.where(sec == 0, 1, east)], ew_r[step][jnp.where(sec == 0, 2, west)])
        z = jnp.where(even, zw_r[step][jnp.where(sec == 0, 1, east)],
                      -zw_r[step][jnp.where(sec == 0, 2, west)])
        value = jnp.where(sec == 0, 0.0, m * (dedge[...] + 0.5 * z)).astype(BF)
        for f in range(F):
            for side, edge, missing, sign in ((0, ROWS - 1, 31, 0.5), (1, 0, 0, -0.5)):
                rows = mr_r[step][side, f * LEV:(f + 1) * LEV, :].astype(F32)
                v = vr_r[step][side].astype(F32)
                term = rows * (diff_v[edge:edge + 1, :] + sign * v) * coef[9, edge:edge + 1, :]
                term = jnp.where(tile == missing, 0.0, term)
                at = pl.ds(f * PLANE + edge, LEV, stride=ROWS)
                put(st, at, wide(st, at) + term)

            @pl.when(sec != 0)
            def _():
                place = edge_pick(LON - 1, 0, f).astype(BF)
                at = pl.ds(f * PLANE, PLANE)
                put(st, at, wide(st, at) + lax.dot_general(value, place, TN, preferred_element_type=F32))

            if done is not None:
                done(f)

    def finish(f):
        at = pl.ds(f * PLANE, PLANE)
        for h in range(2):
            copy = pltpu.make_async_copy(st.at[h, at], out.at[at, pl.ds(h * 128, 128)], out_sem.at[f, h])
            copy.start()
            outs.append(copy)

    outs = []
    loads[0].wait()
    loads[1].wait()
    send_surface(0)
    loads[2].wait()
    for part in (2, 1, 0):
        stage_one(0, part)
    for part in (2, 1, 0):
        stage_one(1, part)
    for load in loads[3:]:
        load.wait()
    prepare()
    couple(0)
    solve()
    send_mixed(0)
    for part in (2, 1, 0):
        stage_two(0, part)
    for part in (0, 2, 1):
        stage_three(0, part)
    for part in (2, 1, 0):
        stage_two(1, part)
    for part in (0, 2, 1):
        assemble(0, part)
    send_velocity(0)
    stencil()
    add_halos(0)
    send_surface(1)
    for part in (0, 2, 1):
        stage_three(1, part)
    couple(1)
    solve()
    send_mixed(1)
    for part in (0, 2, 1):
        assemble(1, part)
    send_velocity(1)
    stencil()
    add_halos(1, finish)
    for copy in outs:
        copy.wait()
    for copy in pending:
        copy.wait_send()


def per_device(adjoint, kappa, diffusion, gain, store, sources, ocean_mask, remap):
    vmem, dma = pltpu.VMEM, pltpu.SemaphoreType.DMA
    both = range(2)

    def each(shape_of):
        return [vmem(shape_of(part), BF) for _ in both for part in range(3)]

    def sizes(part):
        return tuple(SIZE[a] for a in ORDERS[part])

    def s1_shape(part):
        n1, n2, n3 = sizes(part)
        return (n1 - 1, n2, n3, 2, PART_ROWS[part], LON)

    def r1_shape(part):
        n1, n2, n3 = sizes(part)
        return (n2, n1, n3, 2, PART_ROWS[part], LON)

    def s3_shape(part):
        return (sizes(part)[2] - 1, NB, PART_ROWS[part], LON)

    def r3_shape(part):
        return (sizes(part)[2], NB, PART_ROWS[part], LON)

    def twice(shape, kind):
        return [vmem(shape, kind) for _ in both]

    state = F * PLANE
    scratch = [
        vmem((SLOTS, F * LEV, LON), BF), vmem((2, state, 128), F32), vmem((2, state, 128), F32),
        vmem((PLANE, LON), F32), vmem((PLANE, LON), F32), vmem((PLANE, LON), F32), vmem((PLANE, LON), F32),
        vmem((2, 2 * PLANE, 128), F32), vmem((ROWS, LON), F32), vmem((ROWS, LON), jnp.int32),
        vmem((ROWS, LON), jnp.int32), vmem((10, ROWS, LON), F32), vmem((ROWS, PLANE), F32),
        vmem((F * ROWS, LON), F32),
        each(s1_shape), each(r1_shape), each(r1_shape), each(s3_shape), each(r3_shape),
        twice((F * ROWS, LON), F32), twice((4, F * ROWS, LON), F32),
        twice((ROWS, PLANE), F32), twice((4, ROWS, PLANE), F32),
        twice((ROWS, PLANE), F32), twice((4, ROWS, PLANE), F32),
        twice((2, F * LEV, LON), BF), twice((2, F * LEV, LON), BF),
        twice((2, LEV, LON), BF), twice((2, LEV, LON), BF),
        dma((7,)), dma((F, 2)), dma((6,)), dma((54,)), dma((54,)), dma((26,)), dma((26,)),
    ]
    leaves, tree = jax.tree.flatten(scratch)

    def body(*refs):
        head, rest = refs[:9], refs[9:]
        kernel(*head, *jax.tree.unflatten(tree, rest))

    anywhere = pl.BlockSpec(memory_space=pl.ANY)
    scalar = pl.BlockSpec(memory_space=pltpu.SMEM)
    result = pl.pallas_call(
        body,
        out_shape=jax.ShapeDtypeStruct((state, LON), F32),
        in_specs=[anywhere] * 6 + [scalar] * 2,
        out_specs=anywhere,
        scratch_shapes=leaves,
        compiler_params=pltpu.CompilerParams(
            collective_id=0, has_side_effects=True, vmem_limit_bytes=56 * 2**20
        ),
        cost_estimate=pl.CostEstimate(flops=100_000_000, bytes_accessed=10_000_000, transcendentals=0),
    )(
        adjoint.reshape(state, LON), kappa.reshape(PLANE - ROWS, LON), diffusion,
        store.reshape(SLOTS, F * LEV, LON), ocean_mask, remap, gain, sources,
    )
    return result.reshape(F, LEV, ROWS, LON)


def solution(mesh):
    return jax.shard_map(
        per_device,
        mesh=mesh,
        in_specs=(
            P(None, None, "tile", "sec"),
            P(None, "tile", "sec"),
            P("tile", "sec"),
            P(),
            P("sec", "tile", None, None, None),
            P("sec", None),
            P("tile", None),
            P("tile", None),
        ),
        out_specs=P(None, None, "tile", "sec"),
        check_vma=False,
    )
```

```python
import functools

import jax
import jax.numpy as jnp
from jax import lax
from jax.experimental import pallas as pl
from jax.experimental.pallas import tpu as pltpu
from jax.sharding import PartitionSpec as P

F = 4
LEV = 64
ROWS = 8
LON = 256
NB = 8
SLOTS = 32
PLANE = LEV * ROWS
SIZE = {"y": 2, "x": 4, "z": 4}
ORDERS = (("x", "z", "y"), ("z", "y", "x"), ("y", "x", "z"))
GROUPS = 2
DEPTH = LEV // GROUPS
CHUNKS = tuple((order, step, at, rows) for step in range(2) for order, at, rows in (
    (0, 0, 16), (1, 16, 16), (2, 64, 32), (0, 32, 16), (1, 96, 32), (2, 48, 16)))
MESH = pl.DeviceIdType.MESH
BF = jnp.bfloat16
F32 = jnp.float32
NT = (((1,), (1,)), ((), ()))
TN = (((0,), (0,)), ((), ()))


def coords(tile):
    return {"y": tile // 16, "x": (tile // 4) % 4, "z": tile % 4}


def tile_of(at):
    return at["y"] * 16 + at["x"] * 4 + at["z"]


def moved(at, axis, by):
    other = dict(at)
    other[axis] = lax.rem(at[axis] + by, SIZE[axis])
    return other


def rows_of(level):
    return pl.ds(pl.multiple_of(level * ROWS, ROWS), ROWS)


def wide(ref, *at):
    return jnp.concatenate([ref[(0, *at)], ref[(1, *at)]], 1)


def put(ref, value, *at):
    ref[(0, *at)] = value[:, :128]
    ref[(1, *at)] = value[:, 128:]


def kernel(adj, kappa, diff, store, mask, remap, gain, sources, out, *scratch):
    (store_v, st, mx, kap, inv, low, up, vel, diff_v, mask_v, remap_v, coef, dedge, cpl, slots, table,
     s1, r1, r2, s3, r3, surf_s, surf_r, ew_s, ew_r, zw_s, zw_r, mr_s, mr_r, vr_s, vr_r,
     load_sem, top_sem, out_sem, own_sem, e_send, e_recv, h_send, h_recv) = scratch
    tile = lax.axis_index("tile")
    sec = lax.axis_index("sec")
    me = coords(tile)

    def load_half(half, sem):
        part = pl.ds(half * 2 * LEV, 2 * LEV)
        return pltpu.make_async_copy(store.at[:, part], store_v[half], load_sem.at[sem])

    def load_state(g, h):
        return pltpu.make_async_copy(
            adj.at[:, pl.ds(g * DEPTH * ROWS, DEPTH * ROWS), pl.ds(h * 128, 128)], st[g].at[h],
            load_sem.at[8 + 2 * g + h])

    tops = [pltpu.make_async_copy(adj.at[f, pl.ds(0, ROWS)], surf_s[0].at[pl.ds(f * ROWS, ROWS)],
                                  top_sem.at[f]) for f in range(F)]
    for top in tops:
        top.start()
    loads = [
        load_half(0, 0),
        *(load_state(g, h) for g in range(GROUPS) for h in range(2)),
        pltpu.make_async_copy(kappa, kap.at[pl.ds(0, PLANE - ROWS)], load_sem.at[3]),
        pltpu.make_async_copy(diff, diff_v, load_sem.at[4]),
        pltpu.make_async_copy(mask, mask_v, load_sem.at[5]),
        pltpu.make_async_copy(remap, remap_v, load_sem.at[6]),
        load_half(1, 7),
    ]
    for load in loads:
        load.start()

    barrier = pltpu.get_barrier_semaphore()
    greeted = 0
    for axis in ("x", "z", "y"):
        for by in range(1, SIZE[axis]):
            pl.semaphore_signal(barrier, inc=1, device_id={"tile": tile_of(moved(me, axis, by))},
                                device_id_type=MESH)
            greeted += 1
    for by in (1, 31):
        pl.semaphore_signal(barrier, inc=1, device_id={"tile": lax.rem(tile + by, 32)},
                            device_id_type=MESH)
        greeted += 1
    for by in (1, 2, 3):
        pl.semaphore_signal(barrier, inc=1, device_id={"sec": lax.rem(sec + by, 4)},
                            device_id_type=MESH)
        greeted += 1

    def find_slots(reader, _):
        first = jnp.int32(0)
        second = jnp.int32(0)
        for j in range(NB):
            source = sources[0, reader * NB + j]
            second = jnp.where(source // SLOTS == tile, source % SLOTS, second)
            source = sources[0, reader * NB + NB - 1 - j]
            first = jnp.where(source // SLOTS == tile, source % SLOTS, first)
        slots[2 * reader] = first
        slots[2 * reader + 1] = second
        return 0

    lax.fori_loop(0, 32, find_slots, 0)
    pl.semaphore_wait(barrier, greeted)

    def find_blocks():
        for order in range(3):
            axis = ORDERS[order][2]
            for by in range(SIZE[axis]):
                reader = tile_of(moved(me, axis, by))
                holders = [sources[0, reader * NB + j] // SLOTS for j in range(NB)]
                for j in range(NB):
                    rank = jnp.int32(0)
                    for i in range(j):
                        rank = rank + jnp.where(holders[i] == holders[j], 1, 0)
                    table[(order * 4 + by) * NB + j] = holders[j] * 2 + jnp.minimum(rank, 1)

    pending = []
    arrivals = {}
    arrivals_sent = {}

    def send(key, src, dst, send_sem, recv_sem, device):
        copy = pltpu.make_async_remote_copy(src, dst, send_sem, recv_sem, device_id=device,
                                            device_id_type=MESH)
        copy.start()
        pending.append(copy)
        arrivals.setdefault(key, []).append(copy)
        arrivals_sent.setdefault(key, []).append(copy)

    def arrived(key):
        for copy in arrivals.pop(key):
            copy.wait_recv()

    hsem = [0]

    def small(key, src, dst, device):
        n = hsem[0]
        hsem[0] += 1
        send(key, src, dst, h_send.at[n], h_recv.at[n], device)

    def to_sections(key, src, dst):
        for by in (1, 2, 3):
            small(key, src, dst.at[sec], {"sec": lax.rem(sec + by, 4)})

    def to_north_south(key, src, dst):
        small(key, src.at[0], dst.at[0], {"tile": lax.rem(tile + 31, 32)})
        small(key, src.at[1], dst.at[1], {"tile": lax.rem(tile + 1, 32)})

    def sent(key):
        for copy in arrivals_sent.pop(key):
            copy.wait_send()
            pending[:] = [other for other in pending if other is not copy]

    def esem(chunk, stage, by):
        return (chunk * 3 + stage) * 3 + by - 1

    def stage_one(chunk):
        order, half, at, rows = CHUNKS[chunk]
        a1, a2, a3 = ORDERS[order]
        n1, n2, n3 = SIZE[a1], SIZE[a2], SIZE[a3]
        sbuf, rbuf = s1[chunk], r1[chunk]
        for by in list(range(1, n1)) + [0]:
            c1 = lax.rem(me[a1] + by, n1)

            def one_reader(i, _):
                c2, c3 = i // n3, lax.rem(i, n3)
                reader = tile_of({a1: c1, a2: c2, a3: c3})
                for k in range(2):
                    slot = slots[2 * reader + k]
                    block = store_v[half][slot, at:at + rows, :]
                    if by:
                        sbuf[by - 1, c2, c3, k] = block
                    else:
                        rbuf[c2, me[a1], c3, k] = block
                return 0

            lax.fori_loop(0, n2 * n3, one_reader, 0)
            if by:
                n = esem(chunk, 0, by)
                send((chunk, 1), sbuf.at[by - 1], rbuf.at[:, me[a1]], e_send.at[n], e_recv.at[n],
                     {"tile": tile_of(moved(me, a1, by))})

    def stage_two(chunk):
        a1, a2, a3 = ORDERS[CHUNKS[chunk][0]]
        src, dst = r1[chunk], r2[chunk]
        arrived((chunk, 1))
        for by in range(1, SIZE[a2]):
            c2 = lax.rem(me[a2] + by, SIZE[a2])
            n = esem(chunk, 1, by)
            send((chunk, 2), src.at[c2], dst.at[me[a2]], e_send.at[n], e_recv.at[n],
                 {"tile": tile_of(moved(me, a2, by))})
        own = pltpu.make_async_copy(src.at[me[a2]], dst.at[me[a2]], own_sem.at[chunk])
        own.start()
        arrivals[("own", chunk)] = [own]

    def stage_three(chunk):
        order = CHUNKS[chunk][0]
        a1, a2, a3 = ORDERS[order]
        n3 = SIZE[a3]
        src, sbuf, rbuf = r2[chunk], s3[chunk], r3[chunk]
        arrivals.pop(("own", chunk))[0].wait()
        arrived((chunk, 2))
        for by in list(range(1, n3)) + [0]:
            target = moved(me, a3, by)
            reader = tile_of(target)
            for j in range(NB):
                known = table[(order * 4 + by) * NB + j]
                holder = coords(known // 2)
                block = src[holder[a2], holder[a1], target[a3], known % 2]
                if by:
                    sbuf[by - 1, j] = block
                else:
                    rbuf[me[a3], j] = block
            if by:
                n = esem(chunk, 2, by)
                send((chunk, 3), sbuf.at[by - 1], rbuf.at[me[a3]], e_send.at[n], e_recv.at[n],
                     {"tile": reader})

    def assemble(chunk):
        order, half, at, rows = CHUNKS[chunk]
        a3 = ORDERS[order][2]
        arrived((chunk, 3))
        for j in range(NB):
            holder = coords(table[order * 4 * NB + j] // 2)
            block = r3[chunk][holder[a3], j]
            vel[at // LEV, pl.ds(j * LEV + at % LEV, rows), :] = block
            if j in (0, NB - 1) and at >= LEV:
                vr_s[half * GROUPS + (at - LEV) // DEPTH][j // (NB - 1)] = block

    lane = lax.broadcasted_iota(jnp.int32, (ROWS, LON), 1)
    row = lax.broadcasted_iota(jnp.int32, (ROWS, LON), 0)

    def edge_pick(low_lane, high_lane, field=None):
        wanted = jnp.where(row % 2 == 0, low_lane, high_lane)
        pick = lane == wanted
        if field is not None:
            pick = pick & (row // 2 == field)
        return jnp.where(pick, 1.0, 0.0)

    def send_surface(step):
        for f in range(F):
            if step:
                surf_s[step][pl.ds(f * ROWS, ROWS), :] = wide(st[0], f, pl.ds(0, ROWS))
            else:
                tops[f].wait()
        to_sections(("surf", step), surf_s[step], surf_r[step])

    def prepare():
        kap[pl.ds(PLANE - ROWS, ROWS), :] = jnp.zeros((ROWS, LON), F32)

        def level(l, carry):
            g, below = carry
            at = rows_of(l)
            above = kap[at, :]
            p = 1.0 + below * g
            w = 1.0 / (p + above)
            inv[at, :] = w
            low[at, :] = below * w
            up[at, :] = above * w
            return p * w, above

        zero = jnp.zeros((ROWS, LON), F32)
        lax.fori_loop(0, LEV, level, (zero, zero))
        d = diff_v[...]
        is_ocean = sec == 0
        sea = jnp.where(is_ocean, mask_v[...].astype(F32), 1.0)
        east_ok = jnp.where(is_ocean | (lane != 0), 1.0, 0.0)
        west_ok = jnp.where(is_ocean | (lane != LON - 1), 1.0, 0.0)
        north_ok = jnp.where(row != 0, 1.0, 0.0)
        south_ok = jnp.where(row != ROWS - 1, 1.0, 0.0)
        values = (
            pltpu.roll(d, 1, 1) * east_ok, 0.5 * east_ok,
            pltpu.roll(d, LON - 1, 1) * west_ok, 0.5 * west_ok,
            pltpu.roll(d, 1, 0) * north_ok, pltpu.roll(d, ROWS - 1, 0) * south_ok,
            1.0 - 4.0 * d, sea,
        )
        for i, value in enumerate(values):
            for r in range(ROWS):
                coef[i, r] = jnp.broadcast_to(value[r:r + 1], (8, LON))
        tiled = jnp.broadcast_to(d[:, None], (ROWS, DEPTH, LON)).reshape(ROWS * DEPTH, LON)
        dedge[...] = lax.dot_general(edge_pick(LON - 1, 0), tiled, NT,
                                     precision=lax.Precision.HIGHEST, preferred_element_type=F32)

    def couple(step):
        surf_r[step][sec] = surf_s[step][...]
        arrived(("surf", step))
        iota = lax.broadcasted_iota(jnp.int32, (128, LON), 0)

        def parts_of(r):
            cell = remap_v[r:r + 1, :]
            onehot = jnp.where(iota == (cell & 127), 1.0, 0.0).astype(BF)
            high = ((cell >> 11) << 4) + (((cell >> 7) & 1) << 3) + ((cell >> 8) & 7)
            return onehot, high, mask_v[r:r + 1, :].astype(F32)

        @pl.when(sec == 0)
        def _():
            table = jnp.concatenate(
                [surf_r[step][s + 1, f * ROWS:(f + 1) * ROWS, h * 128:(h + 1) * 128]
                 for f in range(F) for s in range(3) for h in range(2)], 0).astype(BF)
            iota48 = lax.broadcasted_iota(jnp.int32, (48, LON), 0)
            for r in range(ROWS):
                onehot, high, sea = parts_of(r)
                found = jnp.dot(table, onehot, preferred_element_type=F32)
                hit = iota48 == high
                for f in range(F):
                    value = jnp.sum(jnp.where(hit, found[f * 48:(f + 1) * 48], 0.0), 0, keepdims=True)
                    cpl[f * ROWS + r:f * ROWS + r + 1, :] = gain[f] * sea * value

        @pl.when(sec != 0)
        def _():
            iota16 = lax.broadcasted_iota(jnp.int32, (16, LON), 0)
            total = jnp.zeros((F * 16, 128), F32)
            for r in range(ROWS):
                onehot, high, sea = parts_of(r)
                hit = iota16 == high - (sec - 1) * 16
                spread = []
                for f in range(F):
                    value = gain[f] * sea * surf_r[step][0, f * ROWS + r:f * ROWS + r + 1, :]
                    spread.append(jnp.where(hit, value, 0.0))
                spread = jnp.concatenate(spread, 0).astype(BF)
                total = total + lax.dot_general(spread, onehot, NT, preferred_element_type=F32)
            for f in range(F):
                for h in range(2):
                    at = (f * 2 + h) * ROWS
                    cpl[f * ROWS:(f + 1) * ROWS, h * 128:(h + 1) * 128] = total[at:at + ROWS]

        for f in range(F):
            at = f, pl.ds(0, ROWS)
            put(st[0], wide(st[0], *at) + cpl[pl.ds(f * ROWS, ROWS), :], *at)

    def eliminate(g):
        def forward(i, carry):
            at = rows_of(g * DEPTH + i)
            w, a = inv[at, :], low[at, :]
            result = []
            for f in range(F):
                d = wide(st[g], f, rows_of(i)) * w + a * carry[f]
                put(st[g], d, f, rows_of(i))
                result.append(d)
            return tuple(result)

        start = tuple(wide(st[g - 1], f, rows_of(DEPTH - 1)) if g else jnp.zeros((ROWS, LON), F32)
                      for f in range(F))
        lax.fori_loop(0, DEPTH, forward, start)

    def substitute():
        later = tuple(jnp.zeros((ROWS, LON), F32) for _ in range(F))
        for g in reversed(range(GROUPS)):
            def backward(i, carry):
                i = DEPTH - 1 - i
                l = g * DEPTH + i
                e = up[rows_of(l), :]
                result = []
                for f in range(F):
                    x = wide(st[g], f, rows_of(i)) + e * carry[f]
                    put(mx, x, pl.ds(f * PLANE + l, ROWS, stride=LEV))
                    result.append(x)
                return tuple(result)

            later = lax.fori_loop(0, DEPTH, backward, later)

    def send_mixed(step):
        for side, edge in ((0, 0), (1, ROWS - 1)):
            for f in range(F):
                mr_s[step][side, f * LEV:(f + 1) * LEV, :] = wide(
                    mx, pl.ds(f * PLANE + edge * LEV, LEV)).astype(BF)
        to_north_south(("mr", step), mr_s[step], mr_r[step])
        for g in range(GROUPS):
            total = jnp.zeros((ROWS, ROWS * DEPTH), F32)
            for f in range(F):
                rows = jnp.concatenate(
                    [wide(mx, pl.ds(f * PLANE + r * LEV + g * DEPTH, DEPTH)) for r in range(ROWS)], 0)
                total = total + lax.dot_general(edge_pick(0, LON - 1, f).astype(BF), rows.astype(BF), NT,
                                                preferred_element_type=F32)
            ew_s[step][g] = total
        to_sections(("ew", step), ew_s[step], ew_r[step])

    def send_velocity(step, g):
        n = step * GROUPS + g
        to_north_south(("vr", n), vr_s[n], vr_r[n])
        rows = jnp.concatenate([vel[0, pl.ds(r * LEV + g * DEPTH, DEPTH), :] for r in range(ROWS)], 0)
        zw_s[n][...] = lax.dot_general(edge_pick(0, LON - 1).astype(BF), rows, NT,
                                       preferred_element_type=F32)
        to_sections(("zw", n), zw_s[n], zw_r[n])

    def stencil(g):
        def tile16(i, _):
            rel = i * 16
            at = g * DEPTH + rel
            for part in range(2):
                lo = at + part * 8
                south = [None] * F
                open_sum = [None] * F
                for r in range(ROWS):
                    here = pl.ds(pl.multiple_of(r * LEV + at, 16), 16)
                    z = vel[0, here, :].astype(F32)[part * 8:part * 8 + 8]
                    v = 0.5 * vel[1, here, :].astype(F32)[part * 8:part * 8 + 8]
                    c_e = coef[0, r] + coef[1, r] * z
                    c_w = coef[2, r] - coef[3, r] * z
                    c_n = coef[4, r] + v
                    c_s = coef[5, r] - v
                    for f in range(F):
                        m = wide(mx, pl.ds(pl.multiple_of(f * PLANE + r * LEV + lo, 8), 8))
                        total = m * coef[6, r]
                        total = total + pltpu.roll(m * c_e, LON - 1, 1)
                        total = total + pltpu.roll(m * c_w, 1, 1)
                        if r:
                            total = total + south[f]
                            put(st[g], (open_sum[f] + m * c_n) * coef[7, r - 1],
                                f, pl.ds((rel + part * 8) * ROWS + r - 1, 8, stride=ROWS))
                        south[f] = m * c_s
                        open_sum[f] = total
                for f in range(F):
                    put(st[g], open_sum[f] * coef[7, ROWS - 1],
                        f, pl.ds((rel + part * 8) * ROWS + ROWS - 1, 8, stride=ROWS))
            return 0

        lax.fori_loop(0, DEPTH // 16, tile16, 0)

    def add_halos(step, g):
        n = step * GROUPS + g
        if g == 0:
            arrived(("mr", step))
            arrived(("ew", step))
        arrived(("vr", n))
        arrived(("zw", n))
        even = lax.broadcasted_iota(jnp.int32, (ROWS, ROWS * DEPTH), 0) % 2 == 0
        east = jnp.where(sec == 0, 1, jnp.where(sec == 3, 1, sec + 1))
        west = jnp.where(sec == 0, 2, jnp.where(sec == 1, 3, sec - 1))
        m = jnp.where(even, ew_r[step][east, g], ew_r[step][west, g])
        z = jnp.where(even, zw_r[n][east], -zw_r[n][west])
        value = jnp.where(sec == 0, 0.0, m * (dedge[...] + 0.5 * z)).astype(BF)
        for f in range(F):
            for side, edge, missing, sign in ((0, ROWS - 1, 31, 0.5), (1, 0, 0, -0.5)):
                rows = mr_r[step][side, f * LEV + g * DEPTH:f * LEV + (g + 1) * DEPTH, :].astype(F32)
                v = vr_r[n][side].astype(F32)
                sea = jnp.where(tile == missing, 0.0, coef[7, edge, 0:1, :])
                term = rows * (diff_v[edge:edge + 1, :] + sign * v) * sea
                at = f, pl.ds(edge, DEPTH, stride=ROWS)
                put(st[g], wide(st[g], *at) + term, *at)

            @pl.when(sec != 0)
            def _():
                place = edge_pick(LON - 1, 0, f).astype(BF)
                add = lax.dot_general(value, place, TN, preferred_element_type=F32)
                for r in range(ROWS):
                    at = f, pl.ds(r, DEPTH, stride=ROWS)
                    put(st[g], wide(st[g], *at) + add[r * DEPTH:(r + 1) * DEPTH], *at)

            if step:
                at = pl.ds(g * DEPTH * ROWS, DEPTH * ROWS)
                for h in range(2):
                    copy = pltpu.make_async_copy(
                        st[g].at[h, f], out.at[f, at, pl.ds(h * 128, 128)], out_sem.at[g, f, h])
                    copy.start()
                    outs.append(copy)

    stages = {"1": stage_one, "2": stage_two, "3": stage_three, "4": assemble}

    def run(*steps):
        for stage, group in (step.split(".") for step in steps):
            for piece in (2, 1, 0):
                stages[stage](int(group) * 3 + piece)

    outs = []
    send_surface(0)
    loads[0].wait()
    run("1.0", "1.1")
    find_blocks()
    for load in loads[1:]:
        load.wait()
    prepare()
    run("2.0", "1.2")
    couple(0)
    eliminate(0)
    eliminate(1)
    substitute()
    send_mixed(0)
    run("2.1", "3.0", "1.3", "2.2", "3.1", "4.0")
    send_velocity(0, 0)
    stencil(0)
    run("2.3", "3.2", "4.1")
    send_velocity(0, 1)
    stencil(1)
    add_halos(0, 0)
    send_surface(1)
    run("3.3")
    add_halos(0, 1)
    couple(1)
    eliminate(0)
    eliminate(1)
    substitute()
    send_mixed(1)
    run("4.2")
    send_velocity(1, 0)
    stencil(0)
    run("4.3")
    send_velocity(1, 1)
    stencil(1)
    add_halos(1, 0)
    add_halos(1, 1)
    for copy in outs:
        copy.wait()
    for copy in pending:
        copy.wait_send()


def per_device(adjoint, kappa, diffusion, gain, store, sources, ocean_mask, remap):
    vmem, dma = pltpu.VMEM, pltpu.SemaphoreType.DMA
    both = range(2)

    def each(lead, count):
        return [vmem(lead(*(SIZE[a] for a in ORDERS[c[0]])) + (count, c[3], LON), BF) for c in CHUNKS]

    def grouped(shape, kind):
        return [vmem(shape, kind) for _ in range(2 * GROUPS)]

    def twice(shape, kind):
        return [vmem(shape, kind) for _ in both]

    scratch = [
        twice((SLOTS, 2 * LEV, LON), BF), [vmem((2, F, DEPTH * ROWS, 128), F32) for _ in range(GROUPS)],
        vmem((2, F * PLANE, 128), F32),
        vmem((PLANE, LON), F32), vmem((PLANE, LON), F32), vmem((PLANE, LON), F32), vmem((PLANE, LON), F32),
        vmem((2, PLANE, LON), BF), vmem((ROWS, LON), F32), vmem((ROWS, LON), jnp.int32),
        vmem((ROWS, LON), jnp.int32), vmem((8, ROWS, 8, LON), F32), vmem((ROWS, ROWS * DEPTH), F32),
        vmem((F * ROWS, LON), F32), pltpu.SMEM((64,), jnp.int32), pltpu.SMEM((96,), jnp.int32),
        each(lambda n1, n2, n3: (n1 - 1, n2, n3), 2), each(lambda n1, n2, n3: (n2, n1, n3), 2),
        each(lambda n1, n2, n3: (n2, n1, n3), 2), each(lambda n1, n2, n3: (n3 - 1,), NB),
        each(lambda n1, n2, n3: (n3,), NB),
        twice((F * ROWS, LON), F32), twice((4, F * ROWS, LON), F32),
        twice((GROUPS, ROWS, ROWS * DEPTH), F32), twice((4, GROUPS, ROWS, ROWS * DEPTH), F32),
        grouped((ROWS, ROWS * DEPTH), F32), grouped((4, ROWS, ROWS * DEPTH), F32),
        twice((2, F * LEV, LON), BF), twice((2, F * LEV, LON), BF),
        grouped((2, DEPTH, LON), BF), grouped((2, DEPTH, LON), BF),
        dma((12,)), dma((F,)), dma((GROUPS, F, 2)), dma((len(CHUNKS),)), dma((9 * len(CHUNKS),)), dma((9 * len(CHUNKS),)), dma((36,)), dma((36,)),
    ]
    leaves, tree = jax.tree.flatten(scratch)

    def body(*refs):
        head, rest = refs[:9], refs[9:]
        kernel(*head, *jax.tree.unflatten(tree, rest))

    anywhere = pl.BlockSpec(memory_space=pl.ANY)
    scalar = pl.BlockSpec(memory_space=pltpu.SMEM)
    result = pl.pallas_call(
        body,
        out_shape=jax.ShapeDtypeStruct((F, PLANE, LON), F32),
        in_specs=[anywhere] * 6 + [scalar] * 2,
        out_specs=anywhere,
        scratch_shapes=leaves,
        compiler_params=pltpu.CompilerParams(
            collective_id=0, has_side_effects=True, vmem_limit_bytes=56 * 2**20
        ),
        cost_estimate=pl.CostEstimate(flops=100_000_000, bytes_accessed=10_000_000, transcendentals=0),
    )(
        adjoint.reshape(F, PLANE, LON), kappa.reshape(PLANE - ROWS, LON), diffusion,
        store.reshape(SLOTS, F * LEV, LON), ocean_mask, remap, gain, sources,
    )
    return result.reshape(F, LEV, ROWS, LON)


def solution(mesh):
    return jax.shard_map(
        per_device,
        mesh=mesh,
        in_specs=(
            P(None, None, "tile", "sec"),
            P(None, "tile", "sec"),
            P("tile", "sec"),
            P(),
            P("sec", "tile", None, None, None),
            P("sec", None),
            P("tile", None),
            P("tile", None),
        ),
        out_specs=P(None, None, "tile", "sec"),
        check_vma=False,
    )
```

```python
import functools

import jax
import jax.numpy as jnp
from jax import lax
from jax.experimental import pallas as pl
from jax.experimental.pallas import tpu as pltpu
from jax.sharding import PartitionSpec as P

F = 4
LEV = 64
ROWS = 8
LON = 256
NB = 8
SLOTS = 32
PLANE = LEV * ROWS
SIZE = {"y": 2, "x": 4, "z": 4}
ORDERS = (("x", "z", "y"), ("z", "y", "x"), ("y", "x", "z"))
GROUPS = 2
DEPTH = LEV // GROUPS
CHUNKS = tuple((order, step, at, rows) for step in range(2) for order, at, rows in (
    (0, 0, 16), (1, 16, 16), (2, 64, 32), (0, 32, 16), (1, 96, 32), (2, 48, 16)))
MESH = pl.DeviceIdType.MESH
BF = jnp.bfloat16
F32 = jnp.float32
NT = (((1,), (1,)), ((), ()))
TN = (((0,), (0,)), ((), ()))


def coords(tile):
    return {"y": tile // 16, "x": (tile // 4) % 4, "z": tile % 4}


def tile_of(at):
    return at["y"] * 16 + at["x"] * 4 + at["z"]


def moved(at, axis, by):
    other = dict(at)
    other[axis] = lax.rem(at[axis] + by, SIZE[axis])
    return other


def rows_of(level):
    return pl.ds(pl.multiple_of(level * ROWS, ROWS), ROWS)


def wide(ref, *at):
    return jnp.concatenate([ref[(0, *at)], ref[(1, *at)]], 1)


def put(ref, value, *at):
    ref[(0, *at)] = value[:, :128]
    ref[(1, *at)] = value[:, 128:]


def kernel(adj, kappa, diff, store, mask, remap, gain, sources, out, *scratch):
    (store_v, st, mx, kap, inv, low, up, vel, diff_v, mask_v, remap_v, coef, dedge, cpl, slots, table,
     s1, r1, r2, s3, r3, surf_s, surf_r, ew_s, ew_r, zw_s, zw_r, mr_s, mr_r, vr_s, vr_r,
     load_sem, top_sem, out_sem, own_sem, e_send, e_recv, h_send, h_recv) = scratch
    tile = lax.axis_index("tile")
    sec = lax.axis_index("sec")
    me = coords(tile)

    def load_half(half, sem):
        part = pl.ds(half * 2 * LEV, 2 * LEV)
        return pltpu.make_async_copy(store.at[:, part], store_v[half], load_sem.at[sem])

    def load_state(g, h):
        return pltpu.make_async_copy(
            adj.at[:, pl.ds(g * DEPTH * ROWS, DEPTH * ROWS), pl.ds(h * 128, 128)], st[g].at[h],
            load_sem.at[8 + 2 * g + h])

    tops = [pltpu.make_async_copy(adj.at[f, pl.ds(0, ROWS)], surf_s[0].at[pl.ds(f * ROWS, ROWS)],
                                  top_sem.at[f]) for f in range(F)]
    for top in tops:
        top.start()
    loads = [
        load_half(0, 0),
        *(load_state(g, h) for g in range(GROUPS) for h in range(2)),
        pltpu.make_async_copy(kappa, kap.at[pl.ds(0, PLANE - ROWS)], load_sem.at[3]),
        pltpu.make_async_copy(diff, diff_v, load_sem.at[4]),
        pltpu.make_async_copy(mask, mask_v, load_sem.at[5]),
        pltpu.make_async_copy(remap, remap_v, load_sem.at[6]),
        load_half(1, 7),
    ]
    for load in loads:
        load.start()

    barrier = pltpu.get_barrier_semaphore()
    greeted = 0
    for axis in ("x", "z", "y"):
        for by in range(1, SIZE[axis]):
            pl.semaphore_signal(barrier, inc=1, device_id={"tile": tile_of(moved(me, axis, by))},
                                device_id_type=MESH)
            greeted += 1
    for by in (1, 31):
        pl.semaphore_signal(barrier, inc=1, device_id={"tile": lax.rem(tile + by, 32)},
                            device_id_type=MESH)
        greeted += 1
    for by in (1, 2, 3):
        pl.semaphore_signal(barrier, inc=1, device_id={"sec": lax.rem(sec + by, 4)},
                            device_id_type=MESH)
        greeted += 1

    def find_slots(reader, _):
        first = jnp.int32(0)
        second = jnp.int32(0)
        for j in range(NB):
            source = sources[0, reader * NB + j]
            second = jnp.where(source // SLOTS == tile, source % SLOTS, second)
            source = sources[0, reader * NB + NB - 1 - j]
            first = jnp.where(source // SLOTS == tile, source % SLOTS, first)
        slots[2 * reader] = first
        slots[2 * reader + 1] = second
        return 0

    lax.fori_loop(0, 32, find_slots, 0)
    pl.semaphore_wait(barrier, greeted)

    def find_blocks():
        for order in range(3):
            axis = ORDERS[order][2]
            for by in range(SIZE[axis]):
                reader = tile_of(moved(me, axis, by))
                holders = [sources[0, reader * NB + j] // SLOTS for j in range(NB)]
                for j in range(NB):
                    rank = jnp.int32(0)
                    for i in range(j):
                        rank = rank + jnp.where(holders[i] == holders[j], 1, 0)
                    table[(order * 4 + by) * NB + j] = holders[j] * 2 + jnp.minimum(rank, 1)

    pending = []
    arrivals = {}
    arrivals_sent = {}

    def send(key, src, dst, send_sem, recv_sem, device):
        copy = pltpu.make_async_remote_copy(src, dst, send_sem, recv_sem, device_id=device,
                                            device_id_type=MESH)
        copy.start()
        pending.append(copy)
        arrivals.setdefault(key, []).append(copy)
        arrivals_sent.setdefault(key, []).append(copy)

    def arrived(key):
        for copy in arrivals.pop(key):
            copy.wait_recv()

    hsem = [0]

    def small(key, src, dst, device):
        n = hsem[0]
        hsem[0] += 1
        send(key, src, dst, h_send.at[n], h_recv.at[n], device)

    def to_sections(key, src, dst):
        for by in (1, 2, 3):
            small(key, src, dst.at[sec], {"sec": lax.rem(sec + by, 4)})

    def to_north_south(key, src, dst):
        small(key, src.at[0], dst.at[0], {"tile": lax.rem(tile + 31, 32)})
        small(key, src.at[1], dst.at[1], {"tile": lax.rem(tile + 1, 32)})

    def sent(key):
        for copy in arrivals_sent.pop(key):
            copy.wait_send()
            pending[:] = [other for other in pending if other is not copy]

    def esem(chunk, stage, by):
        return (chunk * 3 + stage) * 3 + by - 1

    def stage_one(chunk):
        order, half, at, rows = CHUNKS[chunk]
        a1, a2, a3 = ORDERS[order]
        n1, n2, n3 = SIZE[a1], SIZE[a2], SIZE[a3]
        sbuf, rbuf = s1[chunk], r1[chunk]
        for by in list(range(1, n1)) + [0]:
            c1 = lax.rem(me[a1] + by, n1)

            def one_reader(i, _):
                c2, c3 = i // n3, lax.rem(i, n3)
                reader = tile_of({a1: c1, a2: c2, a3: c3})
                for k in range(2):
                    slot = slots[2 * reader + k]
                    block = store_v[half][slot, at:at + rows, :]
                    if by:
                        sbuf[by - 1, c2, c3, k] = block
                    else:
                        rbuf[c2, me[a1], c3, k] = block
                return 0

            lax.fori_loop(0, n2 * n3, one_reader, 0)
            if by:
                n = esem(chunk, 0, by)
                send((chunk, 1), sbuf.at[by - 1], rbuf.at[:, me[a1]], e_send.at[n], e_recv.at[n],
                     {"tile": tile_of(moved(me, a1, by))})

    def stage_two(chunk):
        a1, a2, a3 = ORDERS[CHUNKS[chunk][0]]
        src, dst = r1[chunk], r2[chunk]
        arrived((chunk, 1))
        for by in range(1, SIZE[a2]):
            c2 = lax.rem(me[a2] + by, SIZE[a2])
            n = esem(chunk, 1, by)
            send((chunk, 2), src.at[c2], dst.at[me[a2]], e_send.at[n], e_recv.at[n],
                 {"tile": tile_of(moved(me, a2, by))})
        own = pltpu.make_async_copy(src.at[me[a2]], dst.at[me[a2]], own_sem.at[chunk])
        own.start()
        arrivals[("own", chunk)] = [own]

    def stage_three(chunk):
        order = CHUNKS[chunk][0]
        a1, a2, a3 = ORDERS[order]
        n3 = SIZE[a3]
        src, sbuf, rbuf = r2[chunk], s3[chunk], r3[chunk]
        arrivals.pop(("own", chunk))[0].wait()
        arrived((chunk, 2))
        for by in list(range(1, n3)) + [0]:
            target = moved(me, a3, by)
            reader = tile_of(target)
            for j in range(NB):
                known = table[(order * 4 + by) * NB + j]
                holder = coords(known // 2)
                block = src[holder[a2], holder[a1], target[a3], known % 2]
                if by:
                    sbuf[by - 1, j] = block
                else:
                    rbuf[me[a3], j] = block
            if by:
                n = esem(chunk, 2, by)
                send((chunk, 3), sbuf.at[by - 1], rbuf.at[me[a3]], e_send.at[n], e_recv.at[n],
                     {"tile": reader})

    def assemble(chunk):
        order, half, at, rows = CHUNKS[chunk]
        a3 = ORDERS[order][2]
        arrived((chunk, 3))
        for j in range(NB):
            holder = coords(table[order * 4 * NB + j] // 2)
            block = r3[chunk][holder[a3], j]
            vel[at // LEV, pl.ds(j * LEV + at % LEV, rows), :] = block
            if j in (0, NB - 1) and at >= LEV:
                vr_s[half * GROUPS + (at - LEV) // DEPTH][j // (NB - 1)] = block

    lane = lax.broadcasted_iota(jnp.int32, (ROWS, LON), 1)
    row = lax.broadcasted_iota(jnp.int32, (ROWS, LON), 0)

    def edge_pick(low_lane, high_lane, field=None):
        wanted = jnp.where(row % 2 == 0, low_lane, high_lane)
        pick = lane == wanted
        if field is not None:
            pick = pick & (row // 2 == field)
        return jnp.where(pick, 1.0, 0.0)

    def send_surface(step):
        for f in range(F):
            if step:
                surf_s[step][pl.ds(f * ROWS, ROWS), :] = wide(st[0], f, pl.ds(0, ROWS))
            else:
                tops[f].wait()
        to_sections(("surf", step), surf_s[step], surf_r[step])

    def prepare():
        kap[pl.ds(PLANE - ROWS, ROWS), :] = jnp.zeros((ROWS, LON), F32)

        def level(l, carry):
            g, below = carry
            at = rows_of(l)
            above = kap[at, :]
            p = 1.0 + below * g
            w = 1.0 / (p + above)
            inv[at, :] = w
            low[at, :] = below * w
            up[at, :] = above * w
            return p * w, above

        zero = jnp.zeros((ROWS, LON), F32)
        lax.fori_loop(0, LEV, level, (zero, zero))
        d = diff_v[...]
        is_ocean = sec == 0
        sea = jnp.where(is_ocean, mask_v[...].astype(F32), 1.0)
        east_ok = jnp.where(is_ocean | (lane != 0), 1.0, 0.0)
        west_ok = jnp.where(is_ocean | (lane != LON - 1), 1.0, 0.0)
        north_ok = jnp.where(row != 0, 1.0, 0.0)
        south_ok = jnp.where(row != ROWS - 1, 1.0, 0.0)
        values = (
            pltpu.roll(d, 1, 1) * east_ok, 0.5 * east_ok,
            pltpu.roll(d, LON - 1, 1) * west_ok, 0.5 * west_ok,
            pltpu.roll(d, 1, 0) * north_ok, pltpu.roll(d, ROWS - 1, 0) * south_ok,
            1.0 - 4.0 * d, sea,
        )
        for i, value in enumerate(values):
            for r in range(ROWS):
                coef[i, r] = jnp.broadcast_to(value[r:r + 1], (8, LON))
        tiled = jnp.broadcast_to(d[:, None], (ROWS, DEPTH, LON)).reshape(ROWS * DEPTH, LON)
        dedge[...] = lax.dot_general(edge_pick(LON - 1, 0), tiled, NT,
                                     precision=lax.Precision.HIGHEST, preferred_element_type=F32)

    def couple(step):
        surf_r[step][sec] = surf_s[step][...]
        arrived(("surf", step))
        iota = lax.broadcasted_iota(jnp.int32, (128, LON), 0)

        def parts_of(r):
            cell = remap_v[r:r + 1, :]
            onehot = jnp.where(iota == (cell & 127), 1.0, 0.0).astype(BF)
            high = ((cell >> 11) << 4) + (((cell >> 7) & 1) << 3) + ((cell >> 8) & 7)
            return onehot, high, mask_v[r:r + 1, :].astype(F32)

        @pl.when(sec == 0)
        def _():
            table = jnp.concatenate(
                [surf_r[step][s + 1, f * ROWS:(f + 1) * ROWS, h * 128:(h + 1) * 128]
                 for f in range(F) for s in range(3) for h in range(2)], 0).astype(BF)
            iota48 = lax.broadcasted_iota(jnp.int32, (48, LON), 0)
            for r in range(ROWS):
                onehot, high, sea = parts_of(r)
                found = jnp.dot(table, onehot, preferred_element_type=F32)
                hit = iota48 == high
                for f in range(F):
                    value = jnp.sum(jnp.where(hit, found[f * 48:(f + 1) * 48], 0.0), 0, keepdims=True)
                    cpl[f * ROWS + r:f * ROWS + r + 1, :] = gain[f] * sea * value

        @pl.when(sec != 0)
        def _():
            iota16 = lax.broadcasted_iota(jnp.int32, (16, LON), 0)
            total = jnp.zeros((F * 16, 128), F32)
            for r in range(ROWS):
                onehot, high, sea = parts_of(r)
                hit = iota16 == high - (sec - 1) * 16
                spread = []
                for f in range(F):
                    value = gain[f] * sea * surf_r[step][0, f * ROWS + r:f * ROWS + r + 1, :]
                    spread.append(jnp.where(hit, value, 0.0))
                spread = jnp.concatenate(spread, 0).astype(BF)
                total = total + lax.dot_general(spread, onehot, NT, preferred_element_type=F32)
            for f in range(F):
                for h in range(2):
                    at = (f * 2 + h) * ROWS
                    cpl[f * ROWS:(f + 1) * ROWS, h * 128:(h + 1) * 128] = total[at:at + ROWS]

        for f in range(F):
            at = f, pl.ds(0, ROWS)
            put(st[0], wide(st[0], *at) + cpl[pl.ds(f * ROWS, ROWS), :], *at)

    def eliminate(g):
        def forward(i, carry):
            at = rows_of(g * DEPTH + i)
            w, a = inv[at, :], low[at, :]
            result = []
            for f in range(F):
                d = wide(st[g], f, rows_of(i)) * w + a * carry[f]
                put(st[g], d, f, rows_of(i))
                result.append(d)
            return tuple(result)

        start = tuple(wide(st[g - 1], f, rows_of(DEPTH - 1)) if g else jnp.zeros((ROWS, LON), F32)
                      for f in range(F))
        lax.fori_loop(0, DEPTH, forward, start, unroll=4)

    def substitute():
        later = tuple(jnp.zeros((ROWS, LON), F32) for _ in range(F))
        for g in reversed(range(GROUPS)):
            def backward(i, carry):
                i = DEPTH - 1 - i
                l = g * DEPTH + i
                e = up[rows_of(l), :]
                result = []
                for f in range(F):
                    x = wide(st[g], f, rows_of(i)) + e * carry[f]
                    put(mx, x, pl.ds(f * PLANE + l, ROWS, stride=LEV))
                    result.append(x)
                return tuple(result)

            later = lax.fori_loop(0, DEPTH, backward, later, unroll=4)

    def send_mixed(step):
        for side, edge in ((0, 0), (1, ROWS - 1)):
            for f in range(F):
                mr_s[step][side, f * LEV:(f + 1) * LEV, :] = wide(
                    mx, pl.ds(f * PLANE + edge * LEV, LEV)).astype(BF)
        to_north_south(("mr", step), mr_s[step], mr_r[step])
        for g in range(GROUPS):
            total = jnp.zeros((ROWS, ROWS * DEPTH), F32)
            for f in range(F):
                rows = jnp.concatenate(
                    [wide(mx, pl.ds(f * PLANE + r * LEV + g * DEPTH, DEPTH)) for r in range(ROWS)], 0)
                total = total + lax.dot_general(edge_pick(0, LON - 1, f).astype(BF), rows.astype(BF), NT,
                                                preferred_element_type=F32)
            ew_s[step][g] = total
        to_sections(("ew", step), ew_s[step], ew_r[step])

    def send_velocity(step, g):
        n = step * GROUPS + g
        to_north_south(("vr", n), vr_s[n], vr_r[n])
        rows = jnp.concatenate([vel[0, pl.ds(r * LEV + g * DEPTH, DEPTH), :] for r in range(ROWS)], 0)
        zw_s[n][...] = lax.dot_general(edge_pick(0, LON - 1).astype(BF), rows, NT,
                                       preferred_element_type=F32)
        to_sections(("zw", n), zw_s[n], zw_r[n])

    def stencil(g):
        def tile16(i, _):
            rel = i * 16
            at = g * DEPTH + rel
            for part in range(2):
                lo = at + part * 8
                south = [None] * F
                open_sum = [None] * F
                for r in range(ROWS):
                    here = pl.ds(pl.multiple_of(r * LEV + at, 16), 16)
                    z = vel[0, here, :].astype(F32)[part * 8:part * 8 + 8]
                    v = 0.5 * vel[1, here, :].astype(F32)[part * 8:part * 8 + 8]
                    c_e = coef[0, r] + coef[1, r] * z
                    c_w = coef[2, r] - coef[3, r] * z
                    c_n = coef[4, r] + v
                    c_s = coef[5, r] - v
                    for f in range(F):
                        m = wide(mx, pl.ds(pl.multiple_of(f * PLANE + r * LEV + lo, 8), 8))
                        total = m * coef[6, r]
                        total = total + pltpu.roll(m * c_e, LON - 1, 1)
                        total = total + pltpu.roll(m * c_w, 1, 1)
                        if r:
                            total = total + south[f]
                            put(st[g], (open_sum[f] + m * c_n) * coef[7, r - 1],
                                f, pl.ds((rel + part * 8) * ROWS + r - 1, 8, stride=ROWS))
                        south[f] = m * c_s
                        open_sum[f] = total
                for f in range(F):
                    put(st[g], open_sum[f] * coef[7, ROWS - 1],
                        f, pl.ds((rel + part * 8) * ROWS + ROWS - 1, 8, stride=ROWS))
            return 0

        lax.fori_loop(0, DEPTH // 16, tile16, 0)

    def add_halos(step, g):
        n = step * GROUPS + g
        if g == 0:
            arrived(("mr", step))
            arrived(("ew", step))
        arrived(("vr", n))
        arrived(("zw", n))
        even = lax.broadcasted_iota(jnp.int32, (ROWS, ROWS * DEPTH), 0) % 2 == 0
        east = jnp.where(sec == 0, 1, jnp.where(sec == 3, 1, sec + 1))
        west = jnp.where(sec == 0, 2, jnp.where(sec == 1, 3, sec - 1))
        m = jnp.where(even, ew_r[step][east, g], ew_r[step][west, g])
        z = jnp.where(even, zw_r[n][east], -zw_r[n][west])
        value = jnp.where(sec == 0, 0.0, m * (dedge[...] + 0.5 * z)).astype(BF)
        for f in range(F):
            for side, edge, missing, sign in ((0, ROWS - 1, 31, 0.5), (1, 0, 0, -0.5)):
                rows = mr_r[step][side, f * LEV + g * DEPTH:f * LEV + (g + 1) * DEPTH, :].astype(F32)
                v = vr_r[n][side].astype(F32)
                sea = jnp.where(tile == missing, 0.0, coef[7, edge, 0:1, :])
                term = rows * (diff_v[edge:edge + 1, :] + sign * v) * sea
                at = f, pl.ds(edge, DEPTH, stride=ROWS)
                put(st[g], wide(st[g], *at) + term, *at)

            @pl.when(sec != 0)
            def _():
                place = edge_pick(LON - 1, 0, f).astype(BF)
                add = lax.dot_general(value, place, TN, preferred_element_type=F32)
                for r in range(ROWS):
                    at = f, pl.ds(r, DEPTH, stride=ROWS)
                    put(st[g], wide(st[g], *at) + add[r * DEPTH:(r + 1) * DEPTH], *at)

            if step:
                at = pl.ds(g * DEPTH * ROWS, DEPTH * ROWS)
                for h in range(2):
                    copy = pltpu.make_async_copy(
                        st[g].at[h, f], out.at[f, at, pl.ds(h * 128, 128)], out_sem.at[g, f, h])
                    copy.start()
                    outs.append(copy)

    stages = {"1": stage_one, "2": stage_two, "3": stage_three, "4": assemble}

    def run(*steps):
        for stage, group in (step.split(".") for step in steps):
            for piece in (2, 1, 0):
                stages[stage](int(group) * 3 + piece)

    outs = []
    send_surface(0)
    loads[0].wait()
    run("1.0", "1.1")
    find_blocks()
    for load in loads[1:]:
        load.wait()
    prepare()
    run("2.0", "1.2")
    couple(0)
    eliminate(0)
    eliminate(1)
    substitute()
    send_mixed(0)
    run("2.1", "3.0", "1.3", "2.2", "3.1", "4.0")
    send_velocity(0, 0)
    stencil(0)
    run("2.3", "3.2", "4.1")
    send_velocity(0, 1)
    stencil(1)
    add_halos(0, 0)
    send_surface(1)
    run("3.3")
    add_halos(0, 1)
    couple(1)
    eliminate(0)
    eliminate(1)
    substitute()
    send_mixed(1)
    run("4.2")
    send_velocity(1, 0)
    stencil(0)
    run("4.3")
    send_velocity(1, 1)
    stencil(1)
    add_halos(1, 0)
    add_halos(1, 1)
    for copy in outs:
        copy.wait()
    for copy in pending:
        copy.wait_send()


def per_device(adjoint, kappa, diffusion, gain, store, sources, ocean_mask, remap):
    vmem, dma = pltpu.VMEM, pltpu.SemaphoreType.DMA
    both = range(2)

    def each(lead, count):
        return [vmem(lead(*(SIZE[a] for a in ORDERS[c[0]])) + (count, c[3], LON), BF) for c in CHUNKS]

    def grouped(shape, kind):
        return [vmem(shape, kind) for _ in range(2 * GROUPS)]

    def twice(shape, kind):
        return [vmem(shape, kind) for _ in both]

    scratch = [
        twice((SLOTS, 2 * LEV, LON), BF), [vmem((2, F, DEPTH * ROWS, 128), F32) for _ in range(GROUPS)],
        vmem((2, F * PLANE, 128), F32),
        vmem((PLANE, LON), F32), vmem((PLANE, LON), F32), vmem((PLANE, LON), F32), vmem((PLANE, LON), F32),
        vmem((2, PLANE, LON), BF), vmem((ROWS, LON), F32), vmem((ROWS, LON), jnp.int32),
        vmem((ROWS, LON), jnp.int32), vmem((8, ROWS, 8, LON), F32), vmem((ROWS, ROWS * DEPTH), F32),
        vmem((F * ROWS, LON), F32), pltpu.SMEM((64,), jnp.int32), pltpu.SMEM((96,), jnp.int32),
        each(lambda n1, n2, n3: (n1 - 1, n2, n3), 2), each(lambda n1, n2, n3: (n2, n1, n3), 2),
        each(lambda n1, n2, n3: (n2, n1, n3), 2), each(lambda n1, n2, n3: (n3 - 1,), NB),
        each(lambda n1, n2, n3: (n3,), NB),
        twice((F * ROWS, LON), F32), twice((4, F * ROWS, LON), F32),
        twice((GROUPS, ROWS, ROWS * DEPTH), F32), twice((4, GROUPS, ROWS, ROWS * DEPTH), F32),
        grouped((ROWS, ROWS * DEPTH), F32), grouped((4, ROWS, ROWS * DEPTH), F32),
        twice((2, F * LEV, LON), BF), twice((2, F * LEV, LON), BF),
        grouped((2, DEPTH, LON), BF), grouped((2, DEPTH, LON), BF),
        dma((12,)), dma((F,)), dma((GROUPS, F, 2)), dma((len(CHUNKS),)), dma((9 * len(CHUNKS),)), dma((9 * len(CHUNKS),)), dma((36,)), dma((36,)),
    ]
    leaves, tree = jax.tree.flatten(scratch)

    def body(*refs):
        head, rest = refs[:9], refs[9:]
        kernel(*head, *jax.tree.unflatten(tree, rest))

    anywhere = pl.BlockSpec(memory_space=pl.ANY)
    scalar = pl.BlockSpec(memory_space=pltpu.SMEM)
    result = pl.pallas_call(
        body,
        out_shape=jax.ShapeDtypeStruct((F, PLANE, LON), F32),
        in_specs=[anywhere] * 6 + [scalar] * 2,
        out_specs=anywhere,
        scratch_shapes=leaves,
        compiler_params=pltpu.CompilerParams(
            collective_id=0, has_side_effects=True, vmem_limit_bytes=56 * 2**20
        ),
        cost_estimate=pl.CostEstimate(flops=100_000_000, bytes_accessed=10_000_000, transcendentals=0),
    )(
        adjoint.reshape(F, PLANE, LON), kappa.reshape(PLANE - ROWS, LON), diffusion,
        store.reshape(SLOTS, F * LEV, LON), ocean_mask, remap, gain, sources,
    )
    return result.reshape(F, LEV, ROWS, LON)


def solution(mesh):
    return jax.shard_map(
        per_device,
        mesh=mesh,
        in_specs=(
            P(None, None, "tile", "sec"),
            P(None, "tile", "sec"),
            P("tile", "sec"),
            P(),
            P("sec", "tile", None, None, None),
            P("sec", None),
            P("tile", None),
            P("tile", None),
        ),
        out_specs=P(None, None, "tile", "sec"),
        check_vma=False,
    )
```
